1024 devices in a mesh: ctx: 128 (over x, y, z_lo), tp: 8 (over z_hi, core).
Axes of the slice: x: 8, y: 8, z: 8 (z_hi: 4, z_lo: 2; z = z_hi * 2 + z_lo), core: 2. Of those that a mesh axis runs over, the one named last changes fastest.
Arguments:
- queries: bfloat16 [16384, 4096], P('ctx', 'tp'), may hold values from -128 to 128
- key_rows: bfloat16 [16384, 4096], P('ctx', 'tp'), may hold values from -6 to 6
- value_rows: bfloat16 [16384, 4096], P('ctx', 'tp'), may hold values from -6 to 6
- view_mask: int32 [128, 3], replicated, may hold values from 0 to 1, as said below
- norm_gain: float32 [4096], replicated, may hold values from 0.5 to 1.5
- normed_grad: bfloat16 [16384, 4096], P(('ctx', 'tp')), may hold values from -6 to 6
Outputs:
- normed: bfloat16 [16384, 4096], P(('ctx', 'tp'))
- query_grad: bfloat16 [16384, 4096], P('ctx', 'tp')
- key_grad: bfloat16 [16384, 4096], P('ctx', 'tp')
- value_grad: bfloat16 [16384, 4096], P('ctx', 'tp')
The draws below stay inside these ranges and needn't reach their ends.
Inputs may be any that keep to these rules, and one draw needn't show every extreme that they name: `view_mask`: the blocks form views of consecutive blocks. Block 0 begins a view; otherwise a view begins only at blocks b with b % 4 equal to 2 or 3, and in every group of 4 blocks at least one of these two begins a view. A column is 1 exactly where its key block lies inside the grid of blocks and either is not later than the query block or lies in the query block's view.
All inputs are finite; a program needn't handle non-finite values.
Results may differ from the reference program's by a relative error of at most 0.012.
Values may be sent and summed in bfloat16 or wider, within the bound.
A program may use at most 32 MiB of HBM per device.

```python
import jax
import jax.numpy as jnp
from jax import lax

HEADS = 32
HSZ = 128
D = 4096
TOK_DEV = 128
REACH = 2
VIEW_BLOCKS = 4
BLOCKS = 128
TOKENS = 16384


def paired_rows(key):
    base_keys = jnp.clip(jax.random.normal(jax.random.fold_in(key, 11), (TOKENS, D), jnp.float32), -5.0, 5.0)
    base_queries = jnp.clip(jax.random.normal(jax.random.fold_in(key, 12), (TOKENS, D), jnp.float32), -5.0, 5.0)
    return (base_queries, base_keys)


def draw_queries(key, part):
    return paired_rows(key)[0].astype(jnp.bfloat16)


def draw_key_rows(key, part):
    return paired_rows(key)[1].astype(jnp.bfloat16)


def draw_view_mask(key, part):
    span_blocks = 2 * REACH - 1
    block_ids = jnp.arange(BLOCKS, dtype=jnp.int32)
    groups = BLOCKS // VIEW_BLOCKS
    kinds = jax.random.randint(jax.random.fold_in(key, 21), (groups,), 0, 3)
    block_kind = jnp.repeat(kinds, VIEW_BLOCKS)
    offset = block_ids % VIEW_BLOCKS
    begins = (block_ids == 0) | (offset == 2) & (block_kind != 1) | (offset == 3) & (block_kind != 0)
    starts = jnp.where(begins, 1, 0).astype(jnp.int32)
    view_ids = jnp.cumsum(starts) - 1
    row_ids = block_ids[:, None]
    column_ids = jnp.arange(span_blocks, dtype=jnp.int32)[None, :]
    target = row_ids + column_ids - (REACH - 1)
    inside = (target >= 0) & (target < BLOCKS)
    clipped = jnp.clip(target, 0, BLOCKS - 1)
    same_view = view_ids[clipped] == view_ids[row_ids]
    later = column_ids > REACH - 1
    live = inside & (jnp.logical_not(later) | same_view)
    return jnp.where(live, 1, 0).astype(jnp.int32)


def steps_of(stream_key, dims, shards, smallest, top_value):
    level, own = 1.0, jax.random.fold_in(stream_key, 6)
    for dim, blocks in shards:
        draws = jnp.exp(jax.random.uniform(jax.random.fold_in(own, dim), (blocks,), jnp.float32, smallest / len(shards), top_value / len(shards)))
        level = level * jnp.repeat(draws, dims[dim] // blocks).reshape([-1 if axis == dim else 1 for axis in range(len(dims))])
    return level


def centred(stream_key, extent, spread, most, pieces=(), kind=jnp.bfloat16):
    drawn = jax.random.normal(stream_key, extent, jnp.float32) * spread
    if len(pieces) > 0:
        drawn = steps_of(stream_key, extent, pieces, -0.22, 0.18) * drawn
    return jnp.clip(drawn, min=-most, max=most).astype(kind)


def setup_inputs(seed: int = 0) -> dict:
    arg_keys = jax.random.split(jax.random.key(seed), 7)
    queries = draw_queries(jax.random.fold_in(arg_keys[6], 71), 0)
    key_rows = draw_key_rows(jax.random.fold_in(arg_keys[6], 71), 0)
    value_rows = centred(arg_keys[2], (TOKENS, D), 1.0, 6.0, ((0, 128), (1, 8)))
    view_mask = draw_view_mask(jax.random.fold_in(arg_keys[6], 71), 0)
    norm_gain = jnp.clip(1.0 + 0.1 * jax.random.normal(arg_keys[4], (D,), jnp.float32), 0.5, 1.5)
    normed_grad = centred(arg_keys[5], (TOKENS, D), 1.0, 6.0, ((0, 1024),))
    return dict(queries=queries, key_rows=key_rows, value_rows=value_rows, view_mask=view_mask, norm_gain=norm_gain, normed_grad=normed_grad)


NEGATIVE = -1e+30
EPSILON = 1e-06

def low_round(values):
    return lax.optimization_barrier(values.astype(jnp.bfloat16)).astype(jnp.float32)

def reference(queries, key_rows, value_rows, view_mask, norm_gain, normed_grad):
    span_blocks = 2 * REACH - 1
    rim_rows = (REACH - 1) * TOK_DEV
    score_scale = HSZ ** (-0.5)
    q_heads = queries.reshape(TOKENS, HEADS, HSZ)
    k_heads = key_rows.reshape(TOKENS, HEADS, HSZ)
    v_heads = value_rows.reshape(TOKENS, HEADS, HSZ)
    pad_width = ((rim_rows, rim_rows), (0, 0), (0, 0))
    k_padded = jnp.pad(k_heads, pad_width)
    v_padded = jnp.pad(v_heads, pad_width)
    block_list = jnp.arange(BLOCKS, dtype=jnp.int32)

    def window_probs(which):
        start = (which * TOK_DEV).astype(jnp.int32)
        q_block = lax.dynamic_slice_in_dim(q_heads, start, TOK_DEV, 0)
        k_window = lax.dynamic_slice_in_dim(k_padded, start, span_blocks * TOK_DEV, 0)
        v_window = lax.dynamic_slice_in_dim(v_padded, start, span_blocks * TOK_DEV, 0)
        live = jnp.repeat(view_mask[which], TOK_DEV) > 0
        scores = jnp.einsum('thd,shd->hts', q_block.astype(jnp.float32), k_window.astype(jnp.float32)) * score_scale
        scores = jnp.where(live[None, None, :], scores, NEGATIVE)
        peak = lax.optimization_barrier(jnp.max(scores, -1, keepdims=True))
        log_total = peak + jnp.log(lax.optimization_barrier(jnp.sum(jnp.exp(scores - peak), -1, keepdims=True)))
        return (k_window, v_window, jnp.exp(scores - log_total), log_total[:, :, 0])

    def forward(which):
        k_window, v_window, probs, log_total = window_probs(which)
        out_block = jnp.einsum('hts,shd->thd', low_round(probs), v_window.astype(jnp.float32)).astype(jnp.bfloat16)
        return (out_block, log_total)
    out_blocks, totals = lax.map(forward, block_list)
    attended = out_blocks.reshape(TOKENS, D)
    values_f = attended.astype(jnp.float32)
    inverse = lax.rsqrt(lax.optimization_barrier(jnp.mean(values_f * values_f, -1, keepdims=True)) + EPSILON)
    gain_row = norm_gain.astype(jnp.float32)
    normed = (values_f * inverse * gain_row).astype(jnp.bfloat16)
    upstream = normed_grad.astype(jnp.float32) * gain_row
    inner_mean = lax.optimization_barrier(jnp.mean(upstream * values_f, -1, keepdims=True))
    attended_grad = (inverse * upstream - values_f * inverse * inverse * inverse * inner_mean).astype(jnp.bfloat16)
    grad_heads = attended_grad.reshape(TOKENS, HEADS, HSZ)
    out_heads = attended.reshape(TOKENS, HEADS, HSZ)
    delta = lax.optimization_barrier(jnp.sum(grad_heads.astype(jnp.float32) * out_heads.astype(jnp.float32), -1))

    def query_side(which):
        start = (which * TOK_DEV).astype(jnp.int32)
        k_window, v_window, probs, log_total = window_probs(which)
        grad_block = lax.dynamic_slice_in_dim(grad_heads, start, TOK_DEV, 0)
        delta_block = lax.dynamic_slice_in_dim(delta, start, TOK_DEV, 0).T
        prob_grad = jnp.einsum('thd,shd->hts', grad_block.astype(jnp.float32), v_window.astype(jnp.float32))
        score_grad = low_round(probs * (prob_grad - delta_block[:, :, None]))
        result = jnp.einsum('hts,shd->thd', score_grad, k_window.astype(jnp.float32)) * score_scale
        return result.astype(jnp.bfloat16)
    query_grad = lax.map(query_side, block_list).reshape(TOKENS, D)
    q_padded = jnp.pad(q_heads, pad_width)
    grad_padded = jnp.pad(grad_heads, pad_width)
    total_rows = jnp.transpose(totals, (0, 2, 1)).reshape(TOKENS, HEADS)
    total_padded = jnp.pad(total_rows, ((rim_rows, rim_rows), (0, 0)))
    delta_padded = jnp.pad(delta, ((rim_rows, rim_rows), (0, 0)))
    mask_padded = jnp.pad(view_mask, ((REACH - 1, REACH - 1), (0, 0)))

    def key_side(which):
        start = (which * TOK_DEV).astype(jnp.int32)
        k_block = lax.dynamic_slice_in_dim(k_heads, start, TOK_DEV, 0).astype(jnp.float32)
        v_block = lax.dynamic_slice_in_dim(v_heads, start, TOK_DEV, 0).astype(jnp.float32)
        q_window = lax.dynamic_slice_in_dim(q_padded, start, span_blocks * TOK_DEV, 0).astype(jnp.float32)
        grad_window = lax.dynamic_slice_in_dim(grad_padded, start, span_blocks * TOK_DEV, 0).astype(jnp.float32)
        total_window = lax.dynamic_slice_in_dim(total_padded, start, span_blocks * TOK_DEV, 0).T
        delta_window = lax.dynamic_slice_in_dim(delta_padded, start, span_blocks * TOK_DEV, 0).T
        mask_rows = lax.dynamic_slice_in_dim(mask_padded, which, span_blocks, 0)
        query_live = jnp.repeat(jnp.diagonal(jnp.flip(mask_rows, 1)), TOK_DEV) > 0
        scores = jnp.einsum('qhd,khd->hqk', q_window, k_block) * score_scale
        scores = jnp.where(query_live[None, :, None], scores, NEGATIVE)
        probs = jnp.exp(scores - total_window[:, :, None])
        prob_grad = jnp.einsum('qhd,khd->hqk', grad_window, v_block)
        score_grad = low_round(probs * (prob_grad - delta_window[:, :, None]))
        key_part = (jnp.einsum('hqk,qhd->khd', score_grad, q_window) * score_scale).astype(jnp.bfloat16)
        value_part = jnp.einsum('hqk,qhd->khd', low_round(probs), grad_window).astype(jnp.bfloat16)
        return (key_part, value_part)
    key_parts, value_parts = lax.map(key_side, block_list)
    return (normed, query_grad, key_parts.reshape(TOKENS, D), value_parts.reshape(TOKENS, D))
```

```python
import jax
import jax.numpy as jnp
from jax import lax
from jax.experimental import pallas as pl
from jax.experimental.pallas import tpu as pltpu
from jax.sharding import PartitionSpec as P

HSZ = 128
NEGATIVE = -1e30
EPSILON = 1e-06
MESH = pl.DeviceIdType.MESH
F32 = jnp.float32
BF16 = jnp.bfloat16


def dot_nn(a, b):
    return lax.dot_general(a, b, (((1,), (0,)), ((), ())), preferred_element_type=F32)


def dot_nt(a, b):
    return lax.dot_general(a, b, (((1,), (1,)), ((), ())), preferred_element_type=F32)


def dot_tn(a, b):
    return lax.dot_general(a, b, (((0,), (0,)), ((), ())), preferred_element_type=F32)


def columns_to_rows(columns):
    size = columns[0].shape[0]
    lane = lax.broadcasted_iota(jnp.int32, (size, size), 1)
    packed = jnp.zeros((size, size), F32)
    for i, column in enumerate(columns):
        packed = jnp.where(lane == i, column, packed)
    return jnp.transpose(packed)[0:8]


def rows_to_columns(rows):
    size = rows.shape[1]
    return jnp.transpose(jnp.concatenate([rows] * (size // 8), axis=0))


def make_kernel(blocks, peers, length, heads):
    width = heads * HSZ
    tile = length // peers
    model = width * peers
    scale = HSZ ** (-0.5)

    def kernel(
        q_hbm, k_hbm, v_hbm, mask_ref, gain_hbm, ng_hbm,
        normed_out, dq_out, dk_out, dv_out,
        q_own, k_own, v_own, q_p, k_p, v_p, q_r, k_r, v_r,
        gain, ng, probs, att, do_own, do_p, do_r,
        rows_own, rows_p, rows_r, stats, normed_v, dq_v, dk_v, dv_v,
        local_sem, out_sem, z_send, z_recv, r_send, r_recv,
        ng_send, ng_recv, st_send, st_recv, no_send, no_recv,
    ):
        b = lax.axis_index("ctx")
        t = lax.axis_index("tp")
        side = 1 - 2 * (b % 2)
        partner = b + side
        relay_to = (b + 2 * side + blocks) % blocks
        relay_from = (b - 2 * side + blocks) % blocks
        other = (b - side + blocks) % blocks

        barrier = pltpu.get_barrier_semaphore()
        greeted = [(partner, t), (relay_to, t), (relay_from, t)]
        greeted += [(b, (t + d) % peers) for d in range(1, peers)]
        for who in greeted:
            pl.semaphore_signal(barrier, inc=1, device_id=who, device_id_type=MESH)

        locals_ = []

        def local(src, dst):
            copy = pltpu.make_async_copy(src, dst, local_sem.at[len(locals_)])
            copy.start()
            locals_.append(copy)

        def cols(ref, h):
            return ref.at[:, pl.ds(h * HSZ, HSZ)]

        for h in range(heads):
            local(cols(k_hbm, h), k_own.at[h])
            local(cols(q_hbm, h), q_own.at[h])
            local(cols(v_hbm, h), v_own.at[h])
        local(ng_hbm.at[:, pl.ds(pl.multiple_of(t * width, width), width)],
              ng.at[pl.ds(pl.multiple_of(t * tile, tile), tile), :])
        local(gain_hbm.at[:, pl.ds(pl.multiple_of(t * width, width), width)], gain)

        pl.semaphore_wait(barrier, len(greeted))

        def remote(src, dst, send, recv, who):
            return pltpu.make_async_remote_copy(
                src_ref=src, dst_ref=dst, send_sem=send, recv_sem=recv,
                device_id=who, device_id_type=MESH)

        plan = []
        for h in range(heads):
            plan.append((cols(k_hbm, h), k_p.at[h], k_r.at[h]))
            plan.append((cols(v_hbm, h), v_p.at[h], v_r.at[h]))
        for h in range(heads):
            plan.append((cols(q_hbm, h), q_p.at[h], q_r.at[h]))
        for h in range(heads):
            plan.append((do_own.at[h], do_p.at[h], do_r.at[h]))
        plan.append((rows_own, rows_p, rows_r))
        to_partner = [
            remote(src, mid, z_send.at[i], z_recv.at[i], (partner, t))
            for i, (src, mid, _) in enumerate(plan)
        ]
        relayed = [
            remote(mid, end, r_send.at[i], r_recv.at[i], (relay_to, t))
            for i, (_, mid, end) in enumerate(plan)
        ]

        def pass_on(i):
            to_partner[i].wait_recv()
            relayed[i].start()

        first_q, first_do = 2 * heads, 3 * heads
        row_copy = 4 * heads
        for i in range(2 * heads):
            to_partner[i].start()

        ng_copies = []
        for d in range(1, peers):
            to = (t + d) % peers
            ng_copies.append(remote(
                ng_hbm.at[:, pl.ds(pl.multiple_of(to * width, width), width)],
                ng.at[pl.ds(pl.multiple_of(t * tile, tile), tile), :],
                ng_send.at[d - 1], ng_recv.at[d - 1], (b, to)))
        for copy in ng_copies:
            copy.start()
        for h in range(heads):
            to_partner[first_q + h].start()

        live_p = mask_ref[1 + side, b] > 0
        live_r = mask_ref[1 - side, b] > 0
        from_p = mask_ref[1 - side, partner] > 0
        from_r = mask_ref[1 + side, other] > 0

        for copy in locals_:
            copy.wait()

        lses = []

        def forward(h):
            query = q_own[h]
            own = dot_nt(query, k_own[h]) * scale
            near = jnp.where(live_p, dot_nt(query, k_p[h]) * scale, NEGATIVE)
            far = jnp.where(live_r, dot_nt(query, k_r[h]) * scale, NEGATIVE)
            peak = jnp.max(jnp.maximum(jnp.maximum(own, near), far), -1, keepdims=True)
            own, near, far = jnp.exp(own - peak), jnp.exp(near - peak), jnp.exp(far - peak)
            total = jnp.sum(own + near + far, -1, keepdims=True)
            inv = 1.0 / total
            lses.append(peak + jnp.log(total))
            own, near, far = own * inv, near * inv, far * inv
            probs[h, 0] = own
            probs[h, 1] = near
            probs[h, 2] = far
            out = (
                dot_nn(own.astype(BF16), v_own[h])
                + dot_nn(near.astype(BF16), v_p[h])
                + dot_nn(far.astype(BF16), v_r[h])
            )
            att[h] = out.astype(BF16)

        for h in range(heads):
            pass_on(2 * h)
            pass_on(2 * h + 1)
            if h > 0:
                relayed[2 * h - 2].wait_recv()
                relayed[2 * h - 1].wait_recv()
                forward(h - 1)
        relayed[2 * heads - 2].wait_recv()
        relayed[2 * heads - 1].wait_recv()
        forward(heads - 1)

        for copy in ng_copies:
            copy.wait_recv()

        def upstream(h):
            return ng[:, h * HSZ:(h + 1) * HSZ].astype(F32) * gain[:, h * HSZ:(h + 1) * HSZ]

        square = jnp.zeros((length, HSZ), F32)
        cross = jnp.zeros((length, HSZ), F32)
        for h in range(heads):
            value = att[h].astype(F32)
            square = square + value * value
            cross = cross + upstream(h) * value
        stats[t] = columns_to_rows(
            [jnp.sum(square, -1, keepdims=True), jnp.sum(cross, -1, keepdims=True)])
        st_copies = []
        for d in range(1, peers):
            to = (t + d) % peers
            st_copies.append(remote(
                stats.at[t], stats.at[t], st_send.at[d - 1], st_recv.at[d - 1], (b, to)))
        for copy in st_copies:
            copy.start()

        for h in range(heads):
            pass_on(first_q + h)

        for copy in st_copies:
            copy.wait_recv()
        sums = stats[0]
        for i in range(1, peers):
            sums = sums + stats[i]
        sums = rows_to_columns(sums)
        inverse = lax.rsqrt(sums[:, 0:1] / model + EPSILON)
        pull = inverse * inverse * inverse * (sums[:, 1:2] / model)

        deltas = []
        for h in range(heads):
            value = att[h].astype(F32)
            grad = (inverse * upstream(h) - value * pull).astype(BF16)
            do_own[h] = grad
            to_partner[first_do + h].start()
            deltas.append(jnp.sum(grad.astype(F32) * value, -1, keepdims=True))
        rows_own[...] = columns_to_rows(lses + deltas)
        to_partner[row_copy].start()
        for h in range(heads):
            value = att[h].astype(F32)
            normed_v[:, h * HSZ:(h + 1) * HSZ] = (
                value * inverse * gain[:, h * HSZ:(h + 1) * HSZ]).astype(BF16)
        no_copies = []
        for d in range(1, peers):
            to = (t + d) % peers
            no_copies.append(remote(
                normed_v.at[pl.ds(pl.multiple_of(to * tile, tile), tile), :],
                normed_out.at[:, pl.ds(pl.multiple_of(t * width, width), width)],
                no_send.at[d - 1], no_recv.at[d - 1], (b, to)))
        for copy in no_copies:
            copy.start()
        outs = []

        def store(src, dst):
            copy = pltpu.make_async_copy(src, dst, out_sem.at[len(outs)])
            copy.start()
            outs.append(copy)

        store(normed_v.at[pl.ds(pl.multiple_of(t * tile, tile), tile), :],
              normed_out.at[:, pl.ds(pl.multiple_of(t * width, width), width)])

        dks, dvs = [], []
        for h in range(heads):
            grad = do_own[h]
            ds = []
            for i, values in enumerate((v_own, v_p, v_r)):
                dp = dot_nt(grad, values[h])
                ds.append((probs[h, i] * (dp - deltas[h])).astype(BF16))
            dq = dot_nn(ds[0], k_own[h]) + dot_nn(ds[1], k_p[h]) + dot_nn(ds[2], k_r[h])
            dq_v[:, h * HSZ:(h + 1) * HSZ] = (dq * scale).astype(BF16)
            dk_v[h] = dot_tn(ds[0], q_own[h])
            dv_v[h] = dot_tn(probs[h, 0].astype(BF16), grad)
        store(dq_v, dq_out)

        for h in range(heads):
            pass_on(first_do + h)
        pass_on(row_copy)

        def key_side(h, queries, grads, rows, live):
            score = dot_nt(k_own[h], queries[h]) * scale
            prob = jnp.where(live, jnp.exp(score - rows[h:h + 1, :]), 0.0)
            grad = grads[h]
            dp = dot_nt(v_own[h], grad)
            ds = (prob * (dp - rows[heads + h:heads + h + 1, :])).astype(BF16)
            return dot_nn(ds, queries[h]), dot_nn(prob.astype(BF16), grad)

        for h in range(heads):
            dk, dv = key_side(h, q_p, do_p, rows_p, from_p)
            dk_v[h] += dk
            dv_v[h] += dv
        for h in range(heads):
            relayed[first_q + h].wait_recv()
        relayed[row_copy].wait_recv()
        for h in range(heads):
            relayed[first_do + h].wait_recv()
            dk, dv = key_side(h, q_r, do_r, rows_r, from_r)
            dks.append(((dk_v[h] + dk) * scale).astype(BF16))
            dvs.append((dv_v[h] + dv).astype(BF16))
        dk_b, dv_b = dq_v, normed_v
        for copy in outs:
            copy.wait()
        for copy in no_copies:
            copy.wait_send()
        for h in range(heads):
            dk_b[:, h * HSZ:(h + 1) * HSZ] = dks[h]
            dv_b[:, h * HSZ:(h + 1) * HSZ] = dvs[h]
        outs.clear()
        store(dk_b, dk_out)
        store(dv_b, dv_out)
        for copy in outs:
            copy.wait()
        for copy in no_copies:
            copy.wait_recv()
        for copy in to_partner + relayed + ng_copies + st_copies:
            copy.wait_send()

    return kernel


def attention(blocks, peers, queries, key_rows, value_rows, view_mask, norm_gain, normed_grad):
    length, width = queries.shape
    heads = width // HSZ
    tile, model = normed_grad.shape
    head_block = pltpu.VMEM((heads, length, HSZ), BF16)
    rows = pltpu.VMEM((8, length), F32)
    copies = 4 * heads + 1
    dma = pltpu.SemaphoreType.DMA
    any_ = pl.BlockSpec(memory_space=pltpu.HBM)
    flat = jax.ShapeDtypeStruct((length, width), BF16)
    return pl.pallas_call(
        make_kernel(blocks, peers, length, heads),
        out_shape=(jax.ShapeDtypeStruct((tile, model), BF16), flat, flat, flat),
        in_specs=[any_, any_, any_, pl.BlockSpec(memory_space=pltpu.SMEM), any_, any_],
        out_specs=(any_, any_, any_, any_),
        scratch_shapes=[head_block] * 9
        + [
            pltpu.VMEM((1, width), F32),
            pltpu.VMEM((length, width), BF16),
            pltpu.VMEM((heads, 3, length, length), F32),
        ]
        + [head_block] * 4
        + [rows] * 3
        + [
            pltpu.VMEM((peers, 8, length), F32),
            pltpu.VMEM((length, width), BF16),
            pltpu.VMEM((length, width), BF16),
            pltpu.VMEM((heads, length, HSZ), F32),
            pltpu.VMEM((heads, length, HSZ), F32),
            dma((3 * heads + 2,)),
            dma((4,)),
            dma((copies,)), dma((copies,)), dma((copies,)), dma((copies,)),
        ]
        + [dma((peers - 1,))] * 6,
        compiler_params=pltpu.CompilerParams(
            collective_id=0, has_side_effects=True, vmem_limit_bytes=60 * 1024 * 1024),
        cost_estimate=pl.CostEstimate(
            flops=2 * 22 * heads * length * length * HSZ,
            bytes_accessed=8 * length * width * 2,
            transcendentals=5 * heads * length * length),
    )(queries, key_rows, value_rows, view_mask.T, norm_gain.reshape(1, model), normed_grad)


def solution(mesh):
    blocks, peers = mesh.shape["ctx"], mesh.shape["tp"]

    def per_device(*arrays):
        return attention(blocks, peers, *arrays)

    placed = (P("ctx", "tp"), P("ctx", "tp"), P("ctx", "tp"), P(), P(), P(("ctx", "tp"), None))
    return jax.shard_map(
        per_device,
        mesh=mesh,
        in_specs=placed,
        out_specs=(P(("ctx", "tp"), None), P("ctx", "tp"), P("ctx", "tp"), P("ctx", "tp")),
        check_vma=False,
    )
```

```python
import contextlib

import jax
import jax.numpy as jnp
from jax import lax
from jax.experimental import pallas as pl
from jax.experimental.pallas import tpu as pltpu
from jax.sharding import PartitionSpec as P

HSZ = 128
NEGATIVE = -1e30
EPSILON = 1e-06
MESH = pl.DeviceIdType.MESH
F32 = jnp.float32
BF16 = jnp.bfloat16
NG_AT = 0
Q_AT = 8
scope = contextlib.nullcontext


def dot_nn(a, b):
    return lax.dot_general(a, b, (((1,), (0,)), ((), ())), preferred_element_type=F32)


def dot_nt(a, b):
    return lax.dot_general(a, b, (((1,), (1,)), ((), ())), preferred_element_type=F32)


def dot_tn(a, b):
    return lax.dot_general(a, b, (((0,), (0,)), ((), ())), preferred_element_type=F32)


def columns_to_rows(columns):
    size = columns[0].shape[0]
    lane = lax.broadcasted_iota(jnp.int32, (size, size), 1)
    packed = jnp.zeros((size, size), F32)
    for i, column in enumerate(columns):
        packed = jnp.where(lane == i, column, packed)
    return jnp.transpose(packed)[0:8]


def rows_to_columns(rows):
    size = rows.shape[1]
    return jnp.transpose(jnp.concatenate([rows] * (size // 8), axis=0))


def make_kernel(blocks, peers, length, heads):
    width = heads * HSZ
    tile = length // peers
    model = width * peers
    half = heads // 2
    scale = HSZ ** (-0.5)

    def kernel(
        q_hbm, k_hbm, v_hbm, mask_ref, gain_hbm, ng_hbm,
        normed_out, dq_out, dk_out, dv_out,
        q_own, k_own, v_own, att, do_own, q_p, k_p, v_p, do_p, q_r, k_r, v_r, do_r,
        ng, gain, probs, far_probs, tiles, normed_v, spread,
        lse_own, lse_p, lse_r, row_own, row_p, row_r, stats, dq_v, dk_v, dv_v, dk_f, dv_f,
        local_sem, out_sem, z_send, z_recv, r_send, r_recv, row_send, row_recv,
        ng_send, ng_recv, st_send, st_recv, at_send, at_recv,
    ):
        b = lax.axis_index("ctx")
        t = lax.axis_index("tp")
        side = 1 - 2 * (b % 2)
        partner = b + side
        relay_to = (b + 2 * side + blocks) % blocks
        relay_from = (b - 2 * side + blocks) % blocks
        other = (b - side + blocks) % blocks

        barrier = pltpu.get_barrier_semaphore()
        greeted = [(partner, t), (relay_to, t), (relay_from, t), (other, t)]
        greeted += [(b, (t + d) % peers) for d in range(1, peers)]
        for who in greeted:
            pl.semaphore_signal(barrier, inc=1, device_id=who, device_id_type=MESH)

        locals_ = []

        def local(src, dst):
            copy = pltpu.make_async_copy(src, dst, local_sem.at[len(locals_)])
            copy.start()
            locals_.append(copy)

        def cols(ref, h):
            return ref.at[:, pl.ds(h * HSZ, HSZ)]

        def part(h):
            return slice(h * HSZ, (h + 1) * HSZ)

        my_cols = pl.ds(pl.multiple_of(t * width, width), width)
        my_rows = pl.ds(pl.multiple_of(t * tile, tile), tile)

        for h in range(heads):
            local(cols(k_hbm, h), k_own.at[h])
            local(cols(q_hbm, h), q_own.at[h])
            local(cols(v_hbm, h), v_own.at[h])
        local(ng_hbm.at[:, my_cols], ng.at[my_rows, :])
        local(gain_hbm, gain)

        with scope("barrier_wait"):
            pl.semaphore_wait(barrier, len(greeted))

        def remote(src, dst, send, recv, who):
            return pltpu.make_async_remote_copy(
                src_ref=src, dst_ref=dst, send_sem=send, recv_sem=recv,
                device_id=who, device_id_type=MESH)

        plan = []
        for h in range(heads):
            plan.append((cols(k_hbm, h), k_p.at[h], k_r.at[h]))
            plan.append((cols(v_hbm, h), v_p.at[h], v_r.at[h]))
        for h in range(0, heads, half):
            plan.append(tuple(x.at[pl.ds(h, half)] for x in (q_own, q_p, q_r)))
        for h in range(heads):
            plan.append((do_own.at[h], do_p.at[h], do_r.at[h]))
        to_partner = [
            remote(src, mid, z_send.at[i], z_recv.at[i], (partner, t))
            for i, (src, mid, _) in enumerate(plan)
        ]
        relayed = [
            remote(mid, end, r_send.at[i], r_recv.at[i], (relay_to, t))
            for i, (_, mid, end) in enumerate(plan)
        ]
        kvs = range(2 * heads)
        qs = range(2 * heads, 2 * heads + 2)
        dos = range(2 * heads + 2, 3 * heads + 2)

        def pass_on(i):
            with scope(f"pass_on{i}"):
                to_partner[i].wait_recv()
                relayed[i].start()

        def peer_copies(source, target, send, recv):
            copies = []
            for d in range(1, peers):
                to = (t + d) % peers
                copies.append(remote(source(to), target, send.at[d - 1], recv.at[d - 1], (b, to)))
            return copies

        ng_copies = peer_copies(
            lambda to: ng_hbm.at[:, pl.ds(pl.multiple_of(to * width, width), width)],
            ng.at[my_rows, :], ng_send, ng_recv)
        st_copies = peer_copies(lambda to: stats.at[t, pl.ds(0, 2)], stats.at[t, pl.ds(0, 2)], st_send, st_recv)
        at_copies = peer_copies(
            lambda to: att.at[:, pl.ds(pl.multiple_of(to * tile, tile), tile), :],
            tiles.at[t], at_send, at_recv)
        lse_copies = [
            remote(lse_own, lse_p, row_send.at[0], row_recv.at[0], (partner, t)),
            remote(lse_own, lse_r, row_send.at[1], row_recv.at[1], (other, t)),
        ]
        row_copies = [
            remote(row_own, row_p, row_send.at[2], row_recv.at[2], (partner, t)),
            remote(row_own, row_r, row_send.at[3], row_recv.at[3], (other, t)),
        ]

        def start(copies):
            for copy in copies:
                copy.start()

        for i in kvs:
            to_partner[i].start()
        if NG_AT == 0:
            start(ng_copies)

        live_p = mask_ref[1 + side, b] > 0
        live_r = mask_ref[1 - side, b] > 0
        from_p = mask_ref[1 - side, partner] > 0
        from_r = mask_ref[1 + side, other] > 0

        with scope("locals"):
            for copy in locals_:
                copy.wait()
        for i in kvs:
            pass_on(i)
            if i + 1 == NG_AT:
                start(ng_copies)
            if i + 1 == Q_AT:
                start([to_partner[j] for j in qs])

        lses = []

        def forward(h):
            query = q_own[h]
            own = dot_nt(query, k_own[h]) * scale
            near = jnp.where(live_p, dot_nt(query, k_p[h]) * scale, NEGATIVE)
            far = jnp.where(live_r, dot_nt(query, k_r[h]) * scale, NEGATIVE)
            peak = jnp.max(jnp.maximum(jnp.maximum(own, near), far), -1, keepdims=True)
            own, near, far = jnp.exp(own - peak), jnp.exp(near - peak), jnp.exp(far - peak)
            total = jnp.sum(own + near + far, -1, keepdims=True)
            inv = 1.0 / total
            lses.append(peak + jnp.log(total))
            own, near, far = own * inv, near * inv, far * inv
            probs[h, 0] = own
            probs[h, 1] = near
            probs[h, 2] = far
            out = (
                dot_nn(own.astype(BF16), v_own[h])
                + dot_nn(near.astype(BF16), v_p[h])
                + dot_nn(far.astype(BF16), v_r[h])
            )
            att[h] = out.astype(BF16)

        for h in range(heads):
            with scope(f"wait_kv{h}"):
                relayed[2 * h].wait_recv()
                relayed[2 * h + 1].wait_recv()
            with scope(f"forward{h}"):
                forward(h)

        my_gain = [gain[:, pl.ds(pl.multiple_of(t * width + h * HSZ, HSZ), HSZ)] for h in range(heads)]

        with scope("wait_ng"):
            for copy in ng_copies:
                copy.wait_recv()
        square = jnp.zeros((length, HSZ), F32)
        cross = jnp.zeros((length, HSZ), F32)
        for h in range(heads):
            value = att[h].astype(F32)
            square = square + value * value
            cross = cross + ng[:, part(h)].astype(F32) * my_gain[h] * value
        stats[t] = columns_to_rows(
            [jnp.sum(square, -1, keepdims=True), jnp.sum(cross, -1, keepdims=True)])
        start(st_copies)
        lse_own[...] = columns_to_rows(lses)
        start(lse_copies)
        if Q_AT > 2 * heads:
            start([to_partner[i] for i in qs])
        start(at_copies)

        for i in qs:
            pass_on(i)

        def key_probs(side_index, queries, rows, live):
            for h in range(heads):
                score = dot_nt(k_own[h], queries[h]) * scale
                far_probs[side_index, h] = jnp.where(live, jnp.exp(score - rows[h:h + 1, :]), 0.0)

        with scope("probs_p"):
            lse_copies[0].wait_recv()
            key_probs(0, q_p, lse_p, from_p)
        with scope("wait_stats"):
            for copy in st_copies:
                copy.wait_recv()
        sums = stats[0]
        for i in range(1, peers):
            sums = sums + stats[i]
        sums = rows_to_columns(sums)
        inverse = lax.rsqrt(sums[:, 0:1] / model + EPSILON)
        pull = inverse * inverse * inverse * (sums[:, 1:2] / model)

        with scope("gradient"):
            deltas = []
            for h in range(heads):
                value = att[h].astype(F32)
                up = ng[:, part(h)].astype(F32) * my_gain[h]
                grad = (inverse * up - value * pull).astype(BF16)
                do_own[h] = grad
                deltas.append(jnp.sum(grad.astype(F32) * value, -1, keepdims=True))
            row_own[...] = columns_to_rows(deltas)
            start(row_copies)
            start([to_partner[i] for i in dos])

        outs = []

        def store(src, dst):
            copy = pltpu.make_async_copy(src, dst, out_sem.at[len(outs)])
            copy.start()
            outs.append(copy)

        for h in range(heads):
            with scope(f"own{h}"):
                grad = do_own[h]
                ds = []
                for i, values in enumerate((v_own, v_p, v_r)):
                    dp = dot_nt(grad, values[h])
                    ds.append((probs[h, i] * (dp - deltas[h])).astype(BF16))
                dq = dot_nn(ds[0], k_own[h]) + dot_nn(ds[1], k_p[h]) + dot_nn(ds[2], k_r[h])
                dq_v[:, part(h)] = (dq * scale).astype(BF16)
                dk_f[h] = dot_tn(ds[0], q_own[h])
                dv_f[h] = dot_tn(probs[h, 0].astype(BF16), grad)
        store(dq_v, dq_out)

        def key_side(h, index, queries, grads, rows):
            grad = grads[h]
            prob = far_probs[index, h]
            dp = dot_nt(v_own[h], grad)
            ds = (prob * (dp - rows[h:h + 1, :])).astype(BF16)
            return dot_nn(ds, queries[h]), dot_nn(prob.astype(BF16), grad)

        with scope("probs_r"):
            lse_copies[1].wait_recv()
            for i in qs:
                relayed[i].wait_recv()
            key_probs(1, q_r, lse_r, from_r)

        for i in dos:
            pass_on(i)
        with scope("wait_row_p"):
            row_copies[0].wait_recv()
        for h in range(heads):
            with scope(f"key_p{h}"):
                dk, dv = key_side(h, 0, q_p, do_p, row_p)
                dk_f[h] += dk
                dv_f[h] += dv

        with scope("wait_tiles"):
            for copy in at_copies:
                copy.wait_recv()
        with scope("normed"):
            tiles[t] = att[:, my_rows, :]
            spread[...] = jnp.broadcast_to(inverse, (length, HSZ))
            tile_inverse = spread[my_rows, :]
            for p in range(peers):
                for h in range(heads):
                    c = p * heads + h
                    normed_v[:, part(c)] = (
                        tiles[p, h].astype(F32) * tile_inverse * gain[:, part(c)]).astype(BF16)
            store(normed_v, normed_out)

        with scope("wait_row_r"):
            row_copies[1].wait_recv()
        for h in range(heads):
            with scope(f"wait_do{h}"):
                relayed[dos[h]].wait_recv()
            with scope(f"key_r{h}"):
                dk, dv = key_side(h, 1, q_r, do_r, row_r)
                dk_v[:, part(h)] = ((dk_f[h] + dk) * scale).astype(BF16)
                dv_v[:, part(h)] = (dv_f[h] + dv).astype(BF16)
                if h % 2 == 1:
                    both = slice((h - 1) * HSZ, (h + 1) * HSZ)
                    store(dk_v.at[:, both], dk_out.at[:, both])
                    store(dv_v.at[:, both], dv_out.at[:, both])
        with scope("wait_sends"):
            for copy in to_partner + relayed + ng_copies + st_copies + at_copies + lse_copies + row_copies:
                copy.wait_send()
        with scope("wait_outs"):
            for copy in outs:
                copy.wait()

    return kernel


def attention(blocks, peers, queries, key_rows, value_rows, view_mask, norm_gain, normed_grad):
    length, width = queries.shape
    heads = width // HSZ
    tile, model = normed_grad.shape
    head_block = pltpu.VMEM((heads, length, HSZ), BF16)
    flat_block = pltpu.VMEM((length, width), BF16)
    total_block = pltpu.VMEM((heads, length, HSZ), F32)
    rows = pltpu.VMEM((8, length), F32)
    copies = 3 * heads + 2
    dma = pltpu.SemaphoreType.DMA
    any_ = pl.BlockSpec(memory_space=pl.ANY)
    flat = jax.ShapeDtypeStruct((length, width), BF16)
    return pl.pallas_call(
        make_kernel(blocks, peers, length, heads),
        out_shape=(jax.ShapeDtypeStruct((tile, model), BF16), flat, flat, flat),
        in_specs=[any_, any_, any_, pl.BlockSpec(memory_space=pltpu.SMEM), any_, any_],
        out_specs=(any_, any_, any_, any_),
        scratch_shapes=[head_block] * 13
        + [flat_block]
        + [
            pltpu.VMEM((1, model), F32),
            pltpu.VMEM((heads, 3, length, length), F32),
            pltpu.VMEM((2, heads, length, length), F32),
            pltpu.VMEM((peers, heads, tile, HSZ), BF16),
            pltpu.VMEM((tile, model), BF16),
            pltpu.VMEM((length, HSZ), F32),
        ]
        + [rows] * 6
        + [pltpu.VMEM((peers, 8, length), F32)]
        + [flat_block] * 3
        + [total_block] * 2
        + [
            dma((3 * heads + 2,)),
            dma((heads + 2,)),
            dma((copies,)), dma((copies,)), dma((copies,)), dma((copies,)),
            dma((4,)), dma((4,)),
        ]
        + [dma((peers - 1,))] * 6,
        compiler_params=pltpu.CompilerParams(
            collective_id=0, has_side_effects=True, vmem_limit_bytes=60 * 1024 * 1024),
        cost_estimate=pl.CostEstimate(
            flops=2 * 22 * heads * length * length * HSZ,
            bytes_accessed=8 * length * width * 2,
            transcendentals=5 * heads * length * length),
    )(queries, key_rows, value_rows, view_mask.T, norm_gain.reshape(1, model), normed_grad)


def copy_out(*arrays):
    n = len(arrays)

    def kernel(*refs):
        sources, outs, held, sems = refs[:n], refs[n:2 * n], refs[2 * n:3 * n], refs[3 * n]
        loads = [pltpu.make_async_copy(sources[i], held[i], sems.at[i]) for i in range(n)]
        stores = [pltpu.make_async_copy(held[i], outs[i], sems.at[n + i]) for i in range(n)]
        for copy in loads:
            copy.start()
        for load, copy in zip(loads, stores):
            load.wait()
            copy.start()
        for copy in stores:
            copy.wait()

    any_ = pl.BlockSpec(memory_space=pl.ANY)
    return pl.pallas_call(
        kernel,
        out_shape=tuple(jax.ShapeDtypeStruct(x.shape, x.dtype) for x in arrays),
        in_specs=[any_] * n,
        out_specs=(any_,) * n,
        scratch_shapes=[pltpu.VMEM(x.shape, x.dtype) for x in arrays]
        + [pltpu.SemaphoreType.DMA((2 * n,))],
        compiler_params=pltpu.CompilerParams(vmem_limit_bytes=60 * 1024 * 1024),
    )(*arrays)


def solution(mesh):
    blocks, peers = mesh.shape["ctx"], mesh.shape["tp"]

    def per_device(*arrays):
        return copy_out(*attention(blocks, peers, *arrays))

    placed = (P("ctx", "tp"), P("ctx", "tp"), P("ctx", "tp"), P(), P(), P(("ctx", "tp"), None))
    return jax.shard_map(
        per_device,
        mesh=mesh,
        in_specs=placed,
        out_specs=(P(("ctx", "tp"), None), P("ctx", "tp"), P("ctx", "tp"), P("ctx", "tp")),
        check_vma=False,
    )
```

```python
import contextlib

import jax
import jax.numpy as jnp
from jax import lax
from jax.experimental import pallas as pl
from jax.experimental.pallas import tpu as pltpu
from jax.sharding import PartitionSpec as P

HSZ = 128
NEGATIVE = -1e30
EPSILON = 1e-06
MESH = pl.DeviceIdType.MESH
F32 = jnp.float32
BF16 = jnp.bfloat16
scope = contextlib.nullcontext


def dot_nn(a, b):
    return lax.dot_general(a, b, (((1,), (0,)), ((), ())), preferred_element_type=F32)


def dot_nt(a, b):
    return lax.dot_general(a, b, (((1,), (1,)), ((), ())), preferred_element_type=F32)


def dot_tn(a, b):
    return lax.dot_general(a, b, (((0,), (0,)), ((), ())), preferred_element_type=F32)


def columns_to_rows(columns):
    size = columns[0].shape[0]
    lane = lax.broadcasted_iota(jnp.int32, (size, size), 1)
    packed = jnp.zeros((size, size), F32)
    for i, column in enumerate(columns):
        packed = jnp.where(lane == i, column, packed)
    return jnp.transpose(packed)[0:8]


def rows_to_columns(rows):
    size = rows.shape[1]
    return jnp.transpose(jnp.concatenate([rows] * (size // 8), axis=0))


class Edge:
    def __init__(self, copy, sends, receives):
        self.copy, self.sends, self.receives = copy, sends, receives

    def start(self):
        pl.when(self.sends)(self.copy.start)

    def wait_send(self):
        pl.when(self.sends)(self.copy.wait_send)

    def wait_recv(self):
        pl.when(self.receives)(self.copy.wait_recv)


def make_kernel(blocks, peers, length, heads):
    width = heads * HSZ
    tile = length // peers
    model = width * peers
    half = heads // 2
    scale = HSZ ** (-0.5)

    def kernel(
        q_hbm, k_hbm, v_hbm, mask_ref, gain_hbm, ng_hbm,
        normed_out, dq_out, dk_out, dv_out,
        q_own, k_own, v_own, att, do_own, q_p, k_p, v_p, do_p, q_r, k_r, v_r, do_r,
        ng, gain, probs, far_probs, tiles, spread,
        lse_own, lse_p, lse_r, row_own, row_p, row_r, stats, dk_f, dv_f,
        local_sem, z_send, z_recv, r_send, r_recv, row_send, row_recv,
        ng_send, ng_recv, st_send, st_recv, at_send, at_recv,
    ):
        b = lax.axis_index("ctx")
        t = lax.axis_index("tp")
        side = 1 - 2 * (b % 2)
        partner = b + side
        relay_to = (b + 2 * side + blocks) % blocks
        relay_from = (b - 2 * side + blocks) % blocks
        other = (b - side + blocks) % blocks

        even = side > 0
        has_far = jnp.where(even, b > 0, b < blocks - 1)
        has_next = jnp.where(even, b < blocks - 2, b > 1)

        barrier = pltpu.get_barrier_semaphore()

        def greet(who):
            pl.semaphore_signal(barrier, inc=1, device_id=who, device_id_type=MESH)

        greet((partner, t))

        @pl.when(has_next)
        def _():
            greet((relay_to, t))

        @pl.when(has_far)
        def _():
            greet((relay_from, t))
            greet((other, t))

        for d in range(peers // 2, 0, -1):
            greet((b, (t + d) % peers))
            if 2 * d != peers:
                greet((b, (t + peers - d) % peers))

        locals_ = []

        def local(src, dst):
            copy = pltpu.make_async_copy(src, dst, local_sem.at[len(locals_)])
            copy.start()
            locals_.append(copy)

        def cols(ref, h):
            return ref.at[:, pl.ds(h * HSZ, HSZ)]

        def part(h):
            return slice(h * HSZ, (h + 1) * HSZ)

        my_cols = pl.ds(pl.multiple_of(t * width, width), width)
        my_rows = pl.ds(pl.multiple_of(t * tile, tile), tile)

        with scope("barrier_wait"):
            pl.semaphore_wait(
                barrier, peers + jnp.where(has_next, 1, 0) + jnp.where(has_far, 2, 0))

        def remote(src, dst, send, recv, who):
            return pltpu.make_async_remote_copy(
                src_ref=src, dst_ref=dst, send_sem=send, recv_sem=recv,
                device_id=who, device_id_type=MESH)

        plan = []
        for h in range(heads):
            plan.append((cols(k_hbm, h), k_p.at[h], k_r.at[h]))
        for h in range(heads):
            plan.append((cols(v_hbm, h), v_p.at[h], v_r.at[h]))
        for h in range(0, heads, half):
            plan.append(tuple(x.at[pl.ds(h, half)] for x in (q_own, q_p, q_r)))
        for h in range(heads):
            plan.append((do_own.at[h], do_p.at[h], do_r.at[h]))
        to_partner = [
            remote(src, mid, z_send.at[i], z_recv.at[i], (partner, t))
            for i, (src, mid, _) in enumerate(plan)
        ]
        relayed = [
            Edge(remote(mid, end, r_send.at[i], r_recv.at[i], (relay_to, t)), has_next, has_far)
            for i, (_, mid, end) in enumerate(plan)
        ]
        kvs = range(2 * heads)
        qs = range(2 * heads, 2 * heads + 2)
        dos = range(2 * heads + 2, 3 * heads + 2)

        def pass_on(i):
            with scope(f"pass_on{i}"):
                to_partner[i].wait_recv()
                relayed[i].start()

        farthest_first = sorted(range(1, peers), key=lambda d: -min(d, peers - d))

        def peer_copies(source, target, send, recv):
            copies = []
            for d in farthest_first:
                to = (t + d) % peers
                copies.append(remote(source(to), target, send.at[d - 1], recv.at[d - 1], (b, to)))
            return copies

        ng_copies = peer_copies(
            lambda to: ng_hbm.at[:, pl.ds(pl.multiple_of(to * width, width), width)],
            ng.at[my_rows, :], ng_send, ng_recv)
        st_copies = peer_copies(lambda to: stats.at[t, pl.ds(0, 2)], stats.at[t, pl.ds(0, 2)], st_send, st_recv)
        at_copies = peer_copies(
            lambda to: att.at[:, pl.ds(pl.multiple_of(to * tile, tile), tile), :],
            tiles.at[t], at_send, at_recv)
        lse_copies = [
            remote(lse_own, lse_p, row_send.at[0], row_recv.at[0], (partner, t)),
            Edge(remote(lse_own, lse_r, row_send.at[1], row_recv.at[1], (other, t)), has_far, has_far),
        ]
        row_copies = [
            remote(row_own, row_p, row_send.at[2], row_recv.at[2], (partner, t)),
            Edge(remote(row_own, row_r, row_send.at[3], row_recv.at[3], (other, t)), has_far, has_far),
        ]

        def start(copies):
            for copy in copies:
                copy.start()

        for i in kvs:
            to_partner[i].start()
        start(ng_copies)

        for h in range(heads):
            local(cols(k_hbm, h), k_own.at[h])
            local(cols(q_hbm, h), q_own.at[h])
            local(cols(v_hbm, h), v_own.at[h])
        local(ng_hbm.at[:, my_cols], ng.at[my_rows, :])
        local(gain_hbm, gain)

        @pl.when(jnp.logical_not(has_far))
        def _():
            for ref in (q_r, k_r, v_r, do_r, lse_r, row_r):
                ref[...] = jnp.zeros_like(ref)

        live_p = mask_ref[1 + side, b] > 0
        live_r = mask_ref[1 - side, b] > 0
        from_p = mask_ref[1 - side, partner] > 0
        from_r = mask_ref[1 + side, other] > 0

        with scope("locals"):
            for copy in locals_:
                copy.wait()
        for i in kvs:
            pass_on(i)
        start([to_partner[i] for i in qs])

        lses = []

        def forward(h):
            query = q_own[h]
            own = dot_nt(query, k_own[h]) * scale
            near = jnp.where(live_p, dot_nt(query, k_p[h]) * scale, NEGATIVE)
            far = jnp.where(live_r, dot_nt(query, k_r[h]) * scale, NEGATIVE)
            peak = jnp.max(jnp.maximum(jnp.maximum(own, near), far), -1, keepdims=True)
            own, near, far = jnp.exp(own - peak), jnp.exp(near - peak), jnp.exp(far - peak)
            total = jnp.sum(own + near + far, -1, keepdims=True)
            inv = 1.0 / total
            lses.append(peak + jnp.log(total))
            own, near, far = own * inv, near * inv, far * inv
            probs[h, 0] = own
            probs[h, 1] = near
            probs[h, 2] = far
            dk_f[h] = dot_nn(own.astype(BF16), v_own[h]) + dot_nn(near.astype(BF16), v_p[h])

        for h in range(heads):
            with scope(f"wait_k{h}"):
                relayed[h].wait_recv()
            with scope(f"forward{h}"):
                forward(h)
        for h in range(heads):
            with scope(f"wait_v{h}"):
                relayed[heads + h].wait_recv()
            with scope(f"attend{h}"):
                out = dk_f[h] + dot_nn(probs[h, 2].astype(BF16), v_r[h])
                att[h] = out.astype(BF16)

        my_gain = [gain[:, pl.ds(pl.multiple_of(t * width + h * HSZ, HSZ), HSZ)] for h in range(heads)]

        with scope("wait_ng"):
            for copy in ng_copies:
                copy.wait_recv()
        square = jnp.zeros((length, HSZ), F32)
        cross = jnp.zeros((length, HSZ), F32)
        for h in range(heads):
            value = att[h].astype(F32)
            square = square + value * value
            cross = cross + ng[:, part(h)].astype(F32) * my_gain[h] * value
        stats[t] = columns_to_rows(
            [jnp.sum(square, -1, keepdims=True), jnp.sum(cross, -1, keepdims=True)])
        start(st_copies)
        lse_own[...] = columns_to_rows(lses)
        start(lse_copies)
        start(at_copies)

        for i in qs:
            pass_on(i)

        def key_probs(side_index, queries, rows, live):
            for h in range(heads):
                score = dot_nt(k_own[h], queries[h]) * scale
                far_probs[side_index, h] = jnp.where(live, jnp.exp(score - rows[h:h + 1, :]), 0.0)

        with scope("probs_p"):
            lse_copies[0].wait_recv()
            key_probs(0, q_p, lse_p, from_p)
        with scope("wait_stats"):
            for copy in st_copies:
                copy.wait_recv()
        sums = stats[0]
        for i in range(1, peers):
            sums = sums + stats[i]
        sums = rows_to_columns(sums)
        inverse = lax.rsqrt(sums[:, 0:1] / model + EPSILON)
        pull = inverse * inverse * inverse * (sums[:, 1:2] / model)

        with scope("gradient"):
            deltas = []
            for h in range(heads):
                value = att[h].astype(F32)
                up = ng[:, part(h)].astype(F32) * my_gain[h]
                grad = (inverse * up - value * pull).astype(BF16)
                do_own[h] = grad
                deltas.append(jnp.sum(grad.astype(F32) * value, -1, keepdims=True))
            row_own[...] = columns_to_rows(deltas)
            start(row_copies)
            start([to_partner[i] for i in dos])

        for h in range(heads):
            with scope(f"own{h}"):
                grad = do_own[h]
                ds = []
                for i, values in enumerate((v_own, v_p, v_r)):
                    dp = dot_nt(grad, values[h])
                    ds.append((probs[h, i] * (dp - deltas[h])).astype(BF16))
                dq = dot_nn(ds[0], k_own[h]) + dot_nn(ds[1], k_p[h]) + dot_nn(ds[2], k_r[h])
                dq_out[:, part(h)] = (dq * scale).astype(BF16)
                dk_f[h] = dot_tn(ds[0], q_own[h])
                dv_f[h] = dot_tn(probs[h, 0].astype(BF16), grad)

        def key_side(h, index, queries, grads, rows):
            grad = grads[h]
            prob = far_probs[index, h]
            dp = dot_nt(v_own[h], grad)
            ds = (prob * (dp - rows[h:h + 1, :])).astype(BF16)
            return dot_nn(ds, queries[h]), dot_nn(prob.astype(BF16), grad)

        with scope("probs_r"):
            lse_copies[1].wait_recv()
            for i in qs:
                relayed[i].wait_recv()
            key_probs(1, q_r, lse_r, from_r)

        for i in dos:
            pass_on(i)
        with scope("wait_row_p"):
            row_copies[0].wait_recv()
        for h in range(heads):
            with scope(f"key_p{h}"):
                dk, dv = key_side(h, 0, q_p, do_p, row_p)
                dk_f[h] += dk
                dv_f[h] += dv

        with scope("wait_tiles"):
            for copy in at_copies:
                copy.wait_recv()
        with scope("normed"):
            tiles[t] = att[:, my_rows, :]
            spread[...] = jnp.broadcast_to(inverse, (length, HSZ))
            tile_inverse = spread[my_rows, :]
            for p in range(peers):
                for h in range(heads):
                    c = p * heads + h
                    normed_out[:, part(c)] = (
                        tiles[p, h].astype(F32) * tile_inverse * gain[:, part(c)]).astype(BF16)

        with scope("wait_row_r"):
            row_copies[1].wait_recv()
        for h in range(heads):
            with scope(f"wait_do{h}"):
                relayed[dos[h]].wait_recv()
            with scope(f"key_r{h}"):
                dk, dv = key_side(h, 1, q_r, do_r, row_r)
                dk_out[:, part(h)] = ((dk_f[h] + dk) * scale).astype(BF16)
                dv_out[:, part(h)] = (dv_f[h] + dv).astype(BF16)
        with scope("wait_sends"):
            for copy in to_partner + relayed + ng_copies + st_copies + at_copies + lse_copies + row_copies:
                copy.wait_send()

    return kernel


def attention(blocks, peers, queries, key_rows, value_rows, view_mask, norm_gain, normed_grad):
    length, width = queries.shape
    heads = width // HSZ
    tile, model = normed_grad.shape
    head_block = pltpu.VMEM((heads, length, HSZ), BF16)
    flat_block = pltpu.VMEM((length, width), BF16)
    total_block = pltpu.VMEM((heads, length, HSZ), F32)
    rows = pltpu.VMEM((8, length), F32)
    copies = 3 * heads + 2
    dma = pltpu.SemaphoreType.DMA
    any_ = pl.BlockSpec(memory_space=pl.ANY)
    flat = jax.ShapeDtypeStruct((length, width), BF16)
    return pl.pallas_call(
        make_kernel(blocks, peers, length, heads),
        out_shape=(jax.ShapeDtypeStruct((tile, model), BF16), flat, flat, flat),
        in_specs=[any_, any_, any_, pl.BlockSpec(memory_space=pltpu.SMEM), any_, any_],
        out_specs=(pl.BlockSpec(memory_space=pltpu.VMEM),) * 4,
        scratch_shapes=[head_block] * 13
        + [flat_block]
        + [
            pltpu.VMEM((1, model), F32),
            pltpu.VMEM((heads, 3, length, length), F32),
            pltpu.VMEM((2, heads, length, length), F32),
            pltpu.VMEM((peers, heads, tile, HSZ), BF16),
            pltpu.VMEM((length, HSZ), F32),
        ]
        + [rows] * 6
        + [pltpu.VMEM((peers, 8, length), F32)]
        + [total_block] * 2
        + [
            dma((3 * heads + 2,)),
            dma((copies,)), dma((copies,)), dma((copies,)), dma((copies,)),
            dma((4,)), dma((4,)),
        ]
        + [dma((peers - 1,))] * 6,
        compiler_params=pltpu.CompilerParams(
            collective_id=0, has_side_effects=True, vmem_limit_bytes=55990000),
        cost_estimate=pl.CostEstimate(
            flops=2 * 22 * heads * length * length * HSZ,
            bytes_accessed=8 * length * width * 2,
            transcendentals=5 * heads * length * length),
    )(queries, key_rows, value_rows, view_mask.T, norm_gain.reshape(1, model), normed_grad)


def copy_out(*arrays):
    n = len(arrays)

    def kernel(*refs):
        sources, outs, sems = refs[:n], refs[n:2 * n], refs[2 * n]
        copies = [pltpu.make_async_copy(sources[i], outs[i], sems.at[i]) for i in range(n)]
        for copy in copies:
            copy.start()
        for copy in copies:
            copy.wait()

    any_ = pl.BlockSpec(memory_space=pl.ANY)
    return pl.pallas_call(
        kernel,
        out_shape=tuple(jax.ShapeDtypeStruct(x.shape, x.dtype) for x in arrays),
        in_specs=[any_] * n,
        out_specs=(any_,) * n,
        scratch_shapes=[pltpu.SemaphoreType.DMA((n,))],
        compiler_params=pltpu.CompilerParams(vmem_limit_bytes=4 * 1024 * 1024),
    )(*arrays)


def solution(mesh):
    blocks, peers = mesh.shape["ctx"], mesh.shape["tp"]

    def per_device(*arrays):
        return copy_out(*attention(blocks, peers, *arrays))

    placed = (P("ctx", "tp"), P("ctx", "tp"), P("ctx", "tp"), P(), P(), P(("ctx", "tp"), None))
    return jax.shard_map(
        per_device,
        mesh=mesh,
        in_specs=placed,
        out_specs=(P(("ctx", "tp"), None), P("ctx", "tp"), P("ctx", "tp"), P("ctx", "tp")),
        check_vma=False,
    )
```

```python
import contextlib

import jax
import jax.numpy as jnp
from jax import lax
from jax.experimental import pallas as pl
from jax.experimental.pallas import tpu as pltpu
from jax.sharding import PartitionSpec as P

HSZ = 128
NEGATIVE = -1e30
EPSILON = 1e-06
MESH = pl.DeviceIdType.MESH
F32 = jnp.float32
BF16 = jnp.bfloat16
scope = contextlib.nullcontext


def dot_nn(a, b):
    return lax.dot_general(a, b, (((1,), (0,)), ((), ())), preferred_element_type=F32)


def dot_nt(a, b):
    return lax.dot_general(a, b, (((1,), (1,)), ((), ())), preferred_element_type=F32)


def dot_tn(a, b):
    return lax.dot_general(a, b, (((0,), (0,)), ((), ())), preferred_element_type=F32)


def columns_to_rows(columns):
    size = columns[0].shape[0]
    lane = lax.broadcasted_iota(jnp.int32, (size, size), 1)
    packed = jnp.zeros((size, size), F32)
    for i, column in enumerate(columns):
        packed = jnp.where(lane == i, column, packed)
    return jnp.transpose(packed)[0:8]


def rows_to_columns(rows):
    size = rows.shape[1]
    return jnp.transpose(jnp.concatenate([rows] * (size // 8), axis=0))


class Edge:
    def __init__(self, copy, sends, receives):
        self.copy, self.sends, self.receives = copy, sends, receives

    def start(self):
        pl.when(self.sends)(self.copy.start)

    def wait_send(self):
        pl.when(self.sends)(self.copy.wait_send)

    def wait_recv(self):
        pl.when(self.receives)(self.copy.wait_recv)


def make_kernel(blocks, peers, length, heads):
    width = heads * HSZ
    tile = length // peers
    model = width * peers
    half = heads // 2
    scale = HSZ ** (-0.5)

    def kernel(
        q_hbm, k_hbm, v_hbm, mask_ref, gain_hbm, ng_hbm,
        normed_out, dq_out, dk_out, dv_out,
        q_own, k_own, v_own, att, do_own, q_p, k_p, v_p, do_p, q_r, k_r, v_r, do_r,
        ng, gain, probs, far_probs, tiles, spread,
        lse_own, lse_p, lse_r, row_own, row_p, row_r, stats, dk_f, dv_f,
        local_sem, z_send, z_recv, r_send, r_recv, row_send, row_recv,
        ng_send, ng_recv, st_send, st_recv, at_send, at_recv,
    ):
        b = lax.axis_index("ctx")
        t = lax.axis_index("tp")
        side = 1 - 2 * (b % 2)
        partner = b + side
        relay_to = (b + 2 * side + blocks) % blocks
        relay_from = (b - 2 * side + blocks) % blocks
        other = (b - side + blocks) % blocks

        even = side > 0
        has_far = jnp.where(even, b > 0, b < blocks - 1)
        has_next = jnp.where(even, b < blocks - 2, b > 1)

        barrier = pltpu.get_barrier_semaphore()

        def greet(who):
            pl.semaphore_signal(barrier, inc=1, device_id=who, device_id_type=MESH)

        greet((partner, t))

        @pl.when(has_next)
        def _():
            greet((relay_to, t))

        @pl.when(has_far)
        def _():
            greet((relay_from, t))
            greet((other, t))

        for d in range(peers // 2, 0, -1):
            greet((b, (t + d) % peers))
            if 2 * d != peers:
                greet((b, (t + peers - d) % peers))

        locals_ = []

        def local(src, dst):
            copy = pltpu.make_async_copy(src, dst, local_sem.at[len(locals_)])
            copy.start()
            locals_.append(copy)

        def cols(ref, h):
            return ref.at[:, pl.ds(h * HSZ, HSZ)]

        def part(h):
            return slice(h * HSZ, (h + 1) * HSZ)

        my_cols = pl.ds(pl.multiple_of(t * width, width), width)
        my_rows = pl.ds(pl.multiple_of(t * tile, tile), tile)

        with scope("barrier_wait"):
            pl.semaphore_wait(
                barrier, peers + jnp.where(has_next, 1, 0) + jnp.where(has_far, 2, 0))

        def remote(src, dst, send, recv, who):
            return pltpu.make_async_remote_copy(
                src_ref=src, dst_ref=dst, send_sem=send, recv_sem=recv,
                device_id=who, device_id_type=MESH)

        plan = []
        for h in range(heads):
            plan.append((cols(k_hbm, h), k_p.at[h], k_r.at[h]))
        for h in range(heads):
            plan.append((cols(v_hbm, h), v_p.at[h], v_r.at[h]))
        for h in range(0, heads, half):
            plan.append(tuple(x.at[pl.ds(h, half)] for x in (q_own, q_p, q_r)))
        for h in range(heads):
            plan.append((do_own.at[h], do_p.at[h], do_r.at[h]))
        to_partner = [
            remote(src, mid, z_send.at[i], z_recv.at[i], (partner, t))
            for i, (src, mid, _) in enumerate(plan)
        ]
        relayed = [
            Edge(remote(mid, end, r_send.at[i], r_recv.at[i], (relay_to, t)), has_next, has_far)
            for i, (_, mid, end) in enumerate(plan)
        ]
        kvs = range(2 * heads)
        qs = range(2 * heads, 2 * heads + 2)
        dos = range(2 * heads + 2, 3 * heads + 2)

        def pass_on(i):
            with scope(f"pass_on{i}"):
                to_partner[i].wait_recv()
                relayed[i].start()

        farthest_first = sorted(range(1, peers), key=lambda d: -min(d, peers - d))

        def peer_copies(source, target, send, recv):
            copies = []
            for d in farthest_first:
                to = (t + d) % peers
                copies.append(remote(source(to), target, send.at[d - 1], recv.at[d - 1], (b, to)))
            return copies

        ng_copies = peer_copies(
            lambda to: ng_hbm.at[:, pl.ds(pl.multiple_of(to * width, width), width)],
            ng.at[my_rows, :], ng_send, ng_recv)
        st_copies = peer_copies(lambda to: stats.at[t, pl.ds(0, 2)], stats.at[t, pl.ds(0, 2)], st_send, st_recv)
        at_copies = peer_copies(
            lambda to: att.at[:, pl.ds(pl.multiple_of(to * tile, tile), tile), :],
            tiles.at[t], at_send, at_recv)
        lse_copies = [
            remote(lse_own, lse_p, row_send.at[0], row_recv.at[0], (partner, t)),
            Edge(remote(lse_own, lse_r, row_send.at[1], row_recv.at[1], (other, t)), has_far, has_far),
        ]
        row_copies = [
            remote(row_own, row_p, row_send.at[2], row_recv.at[2], (partner, t)),
            Edge(remote(row_own, row_r, row_send.at[3], row_recv.at[3], (other, t)), has_far, has_far),
        ]

        def start(copies):
            for copy in copies:
                copy.start()

        for i in kvs:
            to_partner[i].start()
        start(ng_copies)

        for h in range(heads):
            local(cols(k_hbm, h), k_own.at[h])
            local(cols(q_hbm, h), q_own.at[h])
            local(cols(v_hbm, h), v_own.at[h])
        local(ng_hbm.at[:, my_cols], ng.at[my_rows, :])
        local(gain_hbm, gain)

        @pl.when(jnp.logical_not(has_far))
        def _():
            for ref in (q_r, k_r, v_r, do_r, lse_r, row_r):
                ref[...] = jnp.zeros_like(ref)

        live_p = mask_ref[1 + side, b] > 0
        live_r = mask_ref[1 - side, b] > 0
        from_p = mask_ref[1 - side, partner] > 0
        from_r = mask_ref[1 + side, other] > 0

        with scope("locals"):
            for copy in locals_:
                copy.wait()
        for i in kvs:
            pass_on(i)
        start([to_partner[i] for i in qs])

        lses = []

        def forward(h):
            query = q_own[h]
            own = dot_nt(query, k_own[h]) * scale
            near = jnp.where(live_p, dot_nt(query, k_p[h]) * scale, NEGATIVE)
            far = jnp.where(live_r, dot_nt(query, k_r[h]) * scale, NEGATIVE)
            peak = jnp.max(jnp.maximum(jnp.maximum(own, near), far), -1, keepdims=True)
            own, near, far = jnp.exp(own - peak), jnp.exp(near - peak), jnp.exp(far - peak)
            total = jnp.sum(own + near + far, -1, keepdims=True)
            inv = 1.0 / total
            lses.append(peak + jnp.log(total))
            own, near, far = own * inv, near * inv, far * inv
            probs[h, 0] = own
            probs[h, 1] = near
            probs[h, 2] = far
            dk_f[h] = dot_nn(own.astype(BF16), v_own[h]) + dot_nn(near.astype(BF16), v_p[h])

        for h in range(heads):
            with scope(f"wait_k{h}"):
                relayed[h].wait_recv()
            with scope(f"forward{h}"):
                forward(h)
        for h in range(heads):
            with scope(f"wait_v{h}"):
                relayed[heads + h].wait_recv()
            with scope(f"attend{h}"):
                out = dk_f[h] + dot_nn(probs[h, 2].astype(BF16), v_r[h])
                att[h] = out.astype(BF16)

        my_gain = [gain[:, pl.ds(pl.multiple_of(t * width + h * HSZ, HSZ), HSZ)] for h in range(heads)]

        square = jnp.zeros((length, HSZ), F32)
        for h in range(heads):
            value = att[h].astype(F32)
            square = square + value * value
        square = jnp.sum(square, -1, keepdims=True)
        with scope("wait_ng"):
            for copy in ng_copies:
                copy.wait_recv()
        cross = jnp.zeros((length, HSZ), F32)
        for h in range(heads):
            cross = cross + ng[:, part(h)].astype(F32) * my_gain[h] * att[h].astype(F32)
        stats[t] = columns_to_rows(
            [square, jnp.sum(cross, -1, keepdims=True)])
        start(st_copies)
        lse_own[...] = columns_to_rows(lses)
        start(lse_copies)
        start(at_copies)

        for i in qs:
            pass_on(i)

        def key_probs(side_index, queries, rows, live):
            for h in range(heads):
                score = dot_nt(k_own[h], queries[h]) * scale
                far_probs[side_index, h] = jnp.where(live, jnp.exp(score - rows[h:h + 1, :]), 0.0)

        with scope("probs_p"):
            lse_copies[0].wait_recv()
            key_probs(0, q_p, lse_p, from_p)
        with scope("wait_stats"):
            for copy in st_copies:
                copy.wait_recv()
        sums = stats[0]
        for i in range(1, peers):
            sums = sums + stats[i]
        sums = rows_to_columns(sums)
        inverse = lax.rsqrt(sums[:, 0:1] / model + EPSILON)
        pull = inverse * inverse * inverse * (sums[:, 1:2] / model)

        with scope("gradient"):
            deltas = []
            for h in range(heads):
                value = att[h].astype(F32)
                up = ng[:, part(h)].astype(F32) * my_gain[h]
                grad = (inverse * up - value * pull).astype(BF16)
                do_own[h] = grad
                deltas.append(jnp.sum(grad.astype(F32) * value, -1, keepdims=True))
            row_own[...] = columns_to_rows(deltas)
            start(row_copies)
            start([to_partner[i] for i in dos])

        for h in range(heads):
            with scope(f"own{h}"):
                grad = do_own[h]
                ds = []
                for i, values in enumerate((v_own, v_p, v_r)):
                    dp = dot_nt(grad, values[h])
                    ds.append((probs[h, i] * (dp - deltas[h])).astype(BF16))
                dq = dot_nn(ds[0], k_own[h]) + dot_nn(ds[1], k_p[h]) + dot_nn(ds[2], k_r[h])
                dq_out[:, part(h)] = (dq * scale).astype(BF16)
                dk_f[h] = dot_tn(ds[0], q_own[h])
                dv_f[h] = dot_tn(probs[h, 0].astype(BF16), grad)

        def key_side(h, index, queries, grads, rows):
            grad = grads[h]
            prob = far_probs[index, h]
            dp = dot_nt(v_own[h], grad)
            ds = (prob * (dp - rows[h:h + 1, :])).astype(BF16)
            return dot_nn(ds, queries[h]), dot_nn(prob.astype(BF16), grad)

        with scope("probs_r"):
            lse_copies[1].wait_recv()
            for i in qs:
                relayed[i].wait_recv()
            key_probs(1, q_r, lse_r, from_r)

        for i in dos:
            pass_on(i)
        with scope("wait_row_p"):
            row_copies[0].wait_recv()
        for h in range(heads):
            with scope(f"key_p{h}"):
                dk, dv = key_side(h, 0, q_p, do_p, row_p)
                dk_f[h] += dk
                dv_f[h] += dv

        with scope("wait_tiles"):
            for copy in at_copies:
                copy.wait_recv()
        with scope("normed"):
            tiles[t] = att[:, my_rows, :]
            spread[...] = jnp.broadcast_to(inverse, (length, HSZ))
            tile_inverse = spread[my_rows, :]
            for p in range(peers):
                for h in range(heads):
                    c = p * heads + h
                    normed_out[:, part(c)] = (
                        tiles[p, h].astype(F32) * tile_inverse * gain[:, part(c)]).astype(BF16)

        with scope("wait_row_r"):
            row_copies[1].wait_recv()
        for h in range(heads):
            with scope(f"wait_do{h}"):
                relayed[dos[h]].wait_recv()
            with scope(f"key_r{h}"):
                dk, dv = key_side(h, 1, q_r, do_r, row_r)
                dk_out[:, part(h)] = ((dk_f[h] + dk) * scale).astype(BF16)
                dv_out[:, part(h)] = (dv_f[h] + dv).astype(BF16)
        with scope("wait_sends"):
            for copy in to_partner + relayed + ng_copies + st_copies + at_copies + lse_copies + row_copies:
                copy.wait_send()

    return kernel


def attention(blocks, peers, queries, key_rows, value_rows, view_mask, norm_gain, normed_grad):
    length, width = queries.shape
    heads = width // HSZ
    tile, model = normed_grad.shape
    head_block = pltpu.VMEM((heads, length, HSZ), BF16)
    flat_block = pltpu.VMEM((length, width), BF16)
    total_block = pltpu.VMEM((heads, length, HSZ), F32)
    rows = pltpu.VMEM((8, length), F32)
    copies = 3 * heads + 2
    dma = pltpu.SemaphoreType.DMA
    hbm = pl.BlockSpec(memory_space=pltpu.HBM)
    flat = jax.ShapeDtypeStruct((length, width), BF16)
    return pl.pallas_call(
        make_kernel(blocks, peers, length, heads),
        out_shape=(jax.ShapeDtypeStruct((tile, model), BF16), flat, flat, flat),
        in_specs=[hbm, hbm, hbm, pl.BlockSpec(memory_space=pltpu.SMEM), hbm, hbm],
        out_specs=(pl.BlockSpec(memory_space=pltpu.VMEM),) * 4,
        scratch_shapes=[head_block] * 13
        + [flat_block]
        + [
            pltpu.VMEM((1, model), F32),
            pltpu.VMEM((heads, 3, length, length), F32),
            pltpu.VMEM((2, heads, length, length), F32),
            pltpu.VMEM((peers, heads, tile, HSZ), BF16),
            pltpu.VMEM((length, HSZ), F32),
        ]
        + [rows] * 6
        + [pltpu.VMEM((peers, 8, length), F32)]
        + [total_block] * 2
        + [
            dma((3 * heads + 2,)),
            dma((copies,)), dma((copies,)), dma((copies,)), dma((copies,)),
            dma((4,)), dma((4,)),
        ]
        + [dma((peers - 1,))] * 6,
        compiler_params=pltpu.CompilerParams(
            collective_id=0, has_side_effects=True, vmem_limit_bytes=55990000),
        cost_estimate=pl.CostEstimate(
            flops=2 * 22 * heads * length * length * HSZ,
            bytes_accessed=8 * length * width * 2,
            transcendentals=5 * heads * length * length),
    )(*(
        pltpu.with_memory_space_constraint(x, pltpu.HBM)
        for x in (
            queries, key_rows, value_rows, view_mask.T, norm_gain.reshape(1, model), normed_grad)
    ))


def copy_out(*arrays):
    n = len(arrays)

    def kernel(*refs):
        sources, outs, sems = refs[:n], refs[n:2 * n], refs[2 * n]
        copies = [pltpu.make_async_copy(sources[i], outs[i], sems.at[i]) for i in range(n)]
        for copy in copies:
            copy.start()
        for copy in copies:
            copy.wait()

    any_ = pl.BlockSpec(memory_space=pl.ANY)
    return pl.pallas_call(
        kernel,
        out_shape=tuple(jax.ShapeDtypeStruct(x.shape, x.dtype) for x in arrays),
        in_specs=[any_] * n,
        out_specs=(any_,) * n,
        scratch_shapes=[pltpu.SemaphoreType.DMA((n,))],
        compiler_params=pltpu.CompilerParams(vmem_limit_bytes=4 * 1024 * 1024),
    )(*arrays)


def solution(mesh):
    blocks, peers = mesh.shape["ctx"], mesh.shape["tp"]

    def per_device(*arrays):
        return copy_out(*attention(blocks, peers, *arrays))

    placed = (P("ctx", "tp"), P("ctx", "tp"), P("ctx", "tp"), P(), P(), P(("ctx", "tp"), None))
    return jax.shard_map(
        per_device,
        mesh=mesh,
        in_specs=placed,
        out_specs=(P(("ctx", "tp"), None), P("ctx", "tp"), P("ctx", "tp"), P("ctx", "tp")),
        check_vma=False,
    )
```

```python
import contextlib

import jax
import jax.numpy as jnp
from jax import lax
from jax.experimental import pallas as pl
from jax.experimental.pallas import tpu as pltpu
from jax.sharding import PartitionSpec as P

HSZ = 128
NEGATIVE = -1e30
EPSILON = 1e-06
MESH = pl.DeviceIdType.MESH
F32 = jnp.float32
BF16 = jnp.bfloat16
scope = contextlib.nullcontext


def dot_nn(a, b):
    return lax.dot_general(a, b, (((1,), (0,)), ((), ())), preferred_element_type=F32)


def dot_nt(a, b):
    return lax.dot_general(a, b, (((1,), (1,)), ((), ())), preferred_element_type=F32)


def dot_tn(a, b):
    return lax.dot_general(a, b, (((0,), (0,)), ((), ())), preferred_element_type=F32)


def columns_to_rows(columns):
    size = columns[0].shape[0]
    lane = lax.broadcasted_iota(jnp.int32, (size, size), 1)
    packed = jnp.zeros((size, size), F32)
    for i, column in enumerate(columns):
        packed = jnp.where(lane == i, column, packed)
    return jnp.transpose(packed)[0:8]


def rows_to_columns(rows):
    size = rows.shape[1]
    return jnp.transpose(jnp.concatenate([rows] * (size // 8), axis=0))


class Edge:
    def __init__(self, copy, sends, receives):
        self.copy, self.sends, self.receives = copy, sends, receives

    def start(self):
        pl.when(self.sends)(self.copy.start)

    def wait_send(self):
        pl.when(self.sends)(self.copy.wait_send)

    def wait_recv(self):
        pl.when(self.receives)(self.copy.wait_recv)


def make_kernel(blocks, peers, length, heads):
    width = heads * HSZ
    tile = length // peers
    model = width * peers
    half = heads // 2
    scale = HSZ ** (-0.5)

    def kernel(
        q_hbm, k_hbm, v_hbm, mask_ref, gain_hbm, ng_hbm,
        normed_out, dq_out, dk_out, dv_out,
        q_own, k_own, v_own, att, do_own, q_p, k_p, v_p, do_p, q_r, k_r, v_r, do_r,
        ng, gain, probs, far_probs, tiles, spread,
        lse_own, lse_p, lse_r, row_own, row_p, row_r, stats, dk_f, dv_f,
        local_sem, z_send, z_recv, r_send, r_recv, row_send, row_recv,
        ng_send, ng_recv, st_send, st_recv, at_send, at_recv,
    ):
        b = lax.axis_index("ctx")
        t = lax.axis_index("tp")
        side = 1 - 2 * (b % 2)
        partner = b + side
        relay_to = (b + 2 * side + blocks) % blocks
        relay_from = (b - 2 * side + blocks) % blocks
        other = (b - side + blocks) % blocks

        even = side > 0
        has_far = jnp.where(even, b > 0, b < blocks - 1)
        has_next = jnp.where(even, b < blocks - 2, b > 1)

        barrier = pltpu.get_barrier_semaphore()

        def greet(who):
            pl.semaphore_signal(barrier, inc=1, device_id=who, device_id_type=MESH)

        greet((partner, t))

        @pl.when(has_next)
        def _():
            greet((relay_to, t))

        @pl.when(has_far)
        def _():
            greet((relay_from, t))
            greet((other, t))

        for d in range(peers // 2, 0, -1):
            greet((b, (t + d) % peers))
            if 2 * d != peers:
                greet((b, (t + peers - d) % peers))

        locals_ = []

        def local(src, dst):
            copy = pltpu.make_async_copy(src, dst, local_sem.at[len(locals_)])
            copy.start()
            locals_.append(copy)

        def cols(ref, h):
            return ref.at[:, pl.ds(h * HSZ, HSZ)]

        def part(h):
            return slice(h * HSZ, (h + 1) * HSZ)

        my_cols = pl.ds(pl.multiple_of(t * width, width), width)
        my_rows = pl.ds(pl.multiple_of(t * tile, tile), tile)

        with scope("barrier_wait"):
            pl.semaphore_wait(
                barrier, peers + jnp.where(has_next, 1, 0) + jnp.where(has_far, 2, 0))

        def remote(src, dst, send, recv, who):
            return pltpu.make_async_remote_copy(
                src_ref=src, dst_ref=dst, send_sem=send, recv_sem=recv,
                device_id=who, device_id_type=MESH)

        plan = []
        for h in range(heads):
            plan.append((cols(k_hbm, h), k_p.at[h], k_r.at[h]))
        for h in range(heads):
            plan.append((cols(v_hbm, h), v_p.at[h], v_r.at[h]))
        for h in range(0, heads, half):
            plan.append(tuple(x.at[pl.ds(h, half)] for x in (q_own, q_p, q_r)))
        for h in range(heads):
            plan.append((do_own.at[h], do_p.at[h], do_r.at[h]))
        to_partner = [
            remote(src, mid, z_send.at[i], z_recv.at[i], (partner, t))
            for i, (src, mid, _) in enumerate(plan)
        ]
        relayed = [
            Edge(remote(mid, end, r_send.at[i], r_recv.at[i], (relay_to, t)), has_next, has_far)
            for i, (_, mid, end) in enumerate(plan)
        ]
        kvs = range(2 * heads)
        qs = range(2 * heads, 2 * heads + 2)
        dos = range(2 * heads + 2, 3 * heads + 2)

        def pass_on(i):
            with scope(f"pass_on{i}"):
                to_partner[i].wait_recv()
                relayed[i].start()

        farthest_first = sorted(range(1, peers), key=lambda d: -min(d, peers - d))

        def peer_copies(source, target, send, recv):
            copies = []
            for d in farthest_first:
                to = (t + d) % peers
                copies.append(remote(source(to), target, send.at[d - 1], recv.at[d - 1], (b, to)))
            return copies

        ng_copies = peer_copies(
            lambda to: ng_hbm.at[:, pl.ds(pl.multiple_of(to * width, width), width)],
            ng.at[my_rows, :], ng_send, ng_recv)
        st_copies = peer_copies(lambda to: stats.at[t, pl.ds(0, 2)], stats.at[t, pl.ds(0, 2)], st_send, st_recv)
        at_copies = peer_copies(
            lambda to: att.at[:, pl.ds(pl.multiple_of(to * tile, tile), tile), :],
            tiles.at[t], at_send, at_recv)
        lse_copies = [
            remote(lse_own, lse_p, row_send.at[0], row_recv.at[0], (partner, t)),
            Edge(remote(lse_own, lse_r, row_send.at[1], row_recv.at[1], (other, t)), has_far, has_far),
        ]
        row_copies = [
            remote(row_own, row_p, row_send.at[2], row_recv.at[2], (partner, t)),
            Edge(remote(row_own, row_r, row_send.at[3], row_recv.at[3], (other, t)), has_far, has_far),
        ]

        def start(copies):
            for copy in copies:
                copy.start()

        for i in kvs:
            to_partner[i].start()
        start(ng_copies)

        for h in range(heads):
            local(cols(k_hbm, h), k_own.at[h])
            local(cols(q_hbm, h), q_own.at[h])
            local(cols(v_hbm, h), v_own.at[h])
        local(ng_hbm.at[:, my_cols], ng.at[my_rows, :])
        local(gain_hbm, gain)

        @pl.when(jnp.logical_not(has_far))
        def _():
            for ref in (q_r, k_r, v_r, do_r, lse_r, row_r):
                ref[...] = jnp.zeros_like(ref)

        live_p = mask_ref[1 + side, b] > 0
        live_r = mask_ref[1 - side, b] > 0
        from_p = mask_ref[1 - side, partner] > 0
        from_r = mask_ref[1 + side, other] > 0

        with scope("locals"):
            for copy in locals_:
                copy.wait()
        for i in kvs:
            pass_on(i)
        start([to_partner[i] for i in qs])

        lses = []

        def forward(h):
            query = q_own[h]
            own = dot_nt(query, k_own[h]) * scale
            near = jnp.where(live_p, dot_nt(query, k_p[h]) * scale, NEGATIVE)
            far = jnp.where(live_r, dot_nt(query, k_r[h]) * scale, NEGATIVE)
            peak = jnp.max(jnp.maximum(jnp.maximum(own, near), far), -1, keepdims=True)
            own, near, far = jnp.exp(own - peak), jnp.exp(near - peak), jnp.exp(far - peak)
            total = jnp.sum(own + near + far, -1, keepdims=True)
            inv = 1.0 / total
            lses.append(peak + jnp.log(total))
            own, near, far = own * inv, near * inv, far * inv
            probs[h, 0] = own
            probs[h, 1] = near
            probs[h, 2] = far
            dk_f[h] = dot_nn(own.astype(BF16), v_own[h]) + dot_nn(near.astype(BF16), v_p[h])

        for h in range(heads):
            with scope(f"wait_k{h}"):
                relayed[h].wait_recv()
            with scope(f"forward{h}"):
                forward(h)
        for h in range(heads):
            with scope(f"wait_v{h}"):
                relayed[heads + h].wait_recv()
            with scope(f"attend{h}"):
                out = dk_f[h] + dot_nn(probs[h, 2].astype(BF16), v_r[h])
                att[h] = out.astype(BF16)

        my_gain = [gain[:, pl.ds(pl.multiple_of(t * width + h * HSZ, HSZ), HSZ)] for h in range(heads)]

        square = jnp.zeros((length, HSZ), F32)
        for h in range(heads):
            value = att[h].astype(F32)
            square = square + value * value
        square = jnp.sum(square, -1, keepdims=True)
        with scope("wait_ng"):
            for copy in ng_copies:
                copy.wait_recv()
        cross = jnp.zeros((length, HSZ), F32)
        for h in range(heads):
            cross = cross + ng[:, part(h)].astype(F32) * my_gain[h] * att[h].astype(F32)
        stats[t] = columns_to_rows(
            [square, jnp.sum(cross, -1, keepdims=True)])
        start(st_copies)
        lse_own[...] = columns_to_rows(lses)
        start(lse_copies)
        start(at_copies)

        for i in qs:
            pass_on(i)

        def key_probs(side_index, queries, rows, live):
            for h in range(heads):
                score = dot_nt(k_own[h], queries[h]) * scale
                far_probs[side_index, h] = jnp.where(live, jnp.exp(score - rows[h:h + 1, :]), 0.0)

        with scope("probs_p"):
            lse_copies[0].wait_recv()
            key_probs(0, q_p, lse_p, from_p)
        with scope("wait_stats"):
            for copy in st_copies:
                copy.wait_recv()
        sums = stats[0]
        for i in range(1, peers):
            sums = sums + stats[i]
        sums = rows_to_columns(sums)
        inverse = lax.rsqrt(sums[:, 0:1] / model + EPSILON)
        pull = inverse * inverse * inverse * (sums[:, 1:2] / model)

        with scope("gradient"):
            deltas = []
            for h in range(heads):
                value = att[h].astype(F32)
                up = ng[:, part(h)].astype(F32) * my_gain[h]
                grad = (inverse * up - value * pull).astype(BF16)
                do_own[h] = grad
                deltas.append(jnp.sum(grad.astype(F32) * value, -1, keepdims=True))
            row_own[...] = columns_to_rows(deltas)
            start(row_copies)
            start([to_partner[i] for i in dos])

        for h in range(heads):
            with scope(f"own{h}"):
                grad = do_own[h]
                ds = []
                for i, values in enumerate((v_own, v_p, v_r)):
                    dp = dot_nt(grad, values[h])
                    ds.append((probs[h, i] * (dp - deltas[h])).astype(BF16))
                dq = dot_nn(ds[0], k_own[h]) + dot_nn(ds[1], k_p[h]) + dot_nn(ds[2], k_r[h])
                dq_out[:, part(h)] = (dq * scale).astype(BF16)
                dk_f[h] = dot_tn(ds[0], q_own[h])
                dv_f[h] = dot_tn(probs[h, 0].astype(BF16), grad)
            if h >= 1:
                for i in ((0,), (1,), (2, 3))[h - 1]:
                    pass_on(dos[i])

        def key_side(h, index, queries, grads, rows):
            grad = grads[h]
            prob = far_probs[index, h]
            dp = dot_nt(v_own[h], grad)
            ds = (prob * (dp - rows[h:h + 1, :])).astype(BF16)
            return dot_nn(ds, queries[h]), dot_nn(prob.astype(BF16), grad)

        with scope("probs_r"):
            lse_copies[1].wait_recv()
            for i in qs:
                relayed[i].wait_recv()
            key_probs(1, q_r, lse_r, from_r)

        with scope("wait_row_p"):
            row_copies[0].wait_recv()
        for h in range(heads):
            with scope(f"key_p{h}"):
                dk, dv = key_side(h, 0, q_p, do_p, row_p)
                dk_f[h] += dk
                dv_f[h] += dv

        with scope("wait_tiles"):
            for copy in at_copies:
                copy.wait_recv()
        with scope("normed"):
            tiles[t] = att[:, my_rows, :]
            spread[...] = jnp.broadcast_to(inverse, (length, HSZ))
            tile_inverse = spread[my_rows, :]
            for p in range(peers):
                for h in range(heads):
                    c = p * heads + h
                    normed_out[:, part(c)] = (
                        tiles[p, h].astype(F32) * tile_inverse * gain[:, part(c)]).astype(BF16)

        with scope("wait_row_r"):
            row_copies[1].wait_recv()
        for h in range(heads):
            with scope(f"wait_do{h}"):
                relayed[dos[h]].wait_recv()
            with scope(f"key_r{h}"):
                dk, dv = key_side(h, 1, q_r, do_r, row_r)
                dk_out[:, part(h)] = ((dk_f[h] + dk) * scale).astype(BF16)
                dv_out[:, part(h)] = (dv_f[h] + dv).astype(BF16)
        with scope("wait_sends"):
            for copy in to_partner + relayed + ng_copies + st_copies + at_copies + lse_copies + row_copies:
                copy.wait_send()

    return kernel


def attention(blocks, peers, queries, key_rows, value_rows, view_mask, norm_gain, normed_grad):
    length, width = queries.shape
    heads = width // HSZ
    tile, model = normed_grad.shape
    head_block = pltpu.VMEM((heads, length, HSZ), BF16)
    flat_block = pltpu.VMEM((length, width), BF16)
    total_block = pltpu.VMEM((heads, length, HSZ), F32)
    rows = pltpu.VMEM((8, length), F32)
    copies = 3 * heads + 2
    dma = pltpu.SemaphoreType.DMA
    hbm = pl.BlockSpec(memory_space=pltpu.HBM)
    flat = jax.ShapeDtypeStruct((length, width), BF16)
    return pl.pallas_call(
        make_kernel(blocks, peers, length, heads),
        out_shape=(jax.ShapeDtypeStruct((tile, model), BF16), flat, flat, flat),
        in_specs=[hbm, hbm, hbm, pl.BlockSpec(memory_space=pltpu.SMEM), hbm, hbm],
        out_specs=(pl.BlockSpec(memory_space=pltpu.VMEM),) * 4,
        scratch_shapes=[head_block] * 13
        + [flat_block]
        + [
            pltpu.VMEM((1, model), F32),
            pltpu.VMEM((heads, 3, length, length), F32),
            pltpu.VMEM((2, heads, length, length), F32),
            pltpu.VMEM((peers, heads, tile, HSZ), BF16),
            pltpu.VMEM((length, HSZ), F32),
        ]
        + [rows] * 6
        + [pltpu.VMEM((peers, 8, length), F32)]
        + [total_block] * 2
        + [
            dma((3 * heads + 2,)),
            dma((copies,)), dma((copies,)), dma((copies,)), dma((copies,)),
            dma((4,)), dma((4,)),
        ]
        + [dma((peers - 1,))] * 6,
        compiler_params=pltpu.CompilerParams(
            collective_id=0, has_side_effects=True, vmem_limit_bytes=55990000),
        cost_estimate=pl.CostEstimate(
            flops=2 * 22 * heads * length * length * HSZ,
            bytes_accessed=8 * length * width * 2,
            transcendentals=5 * heads * length * length),
    )(*(
        pltpu.with_memory_space_constraint(x, pltpu.HBM)
        for x in (
            queries, key_rows, value_rows, view_mask.T, norm_gain.reshape(1, model), normed_grad)
    ))


def copy_out(*arrays):
    n = len(arrays)

    def kernel(*refs):
        sources, outs, sems = refs[:n], refs[n:2 * n], refs[2 * n]
        copies = [pltpu.make_async_copy(sources[i], outs[i], sems.at[i]) for i in range(n)]
        for copy in copies:
            copy.start()
        for copy in copies:
            copy.wait()

    any_ = pl.BlockSpec(memory_space=pl.ANY)
    return pl.pallas_call(
        kernel,
        out_shape=tuple(jax.ShapeDtypeStruct(x.shape, x.dtype) for x in arrays),
        in_specs=[any_] * n,
        out_specs=(any_,) * n,
        scratch_shapes=[pltpu.SemaphoreType.DMA((n,))],
        compiler_params=pltpu.CompilerParams(vmem_limit_bytes=4 * 1024 * 1024),
    )(*arrays)


def solution(mesh):
    blocks, peers = mesh.shape["ctx"], mesh.shape["tp"]

    def per_device(*arrays):
        return copy_out(*attention(blocks, peers, *arrays))

    placed = (P("ctx", "tp"), P("ctx", "tp"), P("ctx", "tp"), P(), P(), P(("ctx", "tp"), None))
    return jax.shard_map(
        per_device,
        mesh=mesh,
        in_specs=placed,
        out_specs=(P(("ctx", "tp"), None), P("ctx", "tp"), P("ctx", "tp"), P("ctx", "tp")),
        check_vma=False,
    )
```
